256 devices in a mesh: ctx: 32 (over z, x), head: 8 (over y, core).
Axes of the slice: x: 4, y: 4, z: 8, core: 2. Of those that a mesh axis runs over, the one named last changes fastest.
Arguments:
- hidden_rows: bfloat16 [8192, 8192], P('ctx', 'head'), may hold values from -6 to 6
- kv_weight: bfloat16 [8192, 2048], P(None, 'head'), may hold values from -0.0625 to 0.0625
- queries: bfloat16 [8192, 8192], P('ctx', 'head')
- kv_pool: bfloat16 [16384, 2048], P('ctx', 'head'), may hold values from -6 to 6
- slot_span: int32 [32], replicated, may hold values from 0 to 31, each once
- span_place: int32 [32], replicated, may hold values from 0 to 15, as said below
- row_index: int32 [32, 256], replicated, may hold values from 0 to 511, as said below
- block_count: int32 [32], replicated, may hold values from 1 to 2, as said below
Outputs:
- fresh_kv: bfloat16 [8192, 2048], P('ctx', 'head')
- attended: bfloat16 [8192, 8192], P('ctx', 'head')
The draws below stay inside these ranges and needn't reach their ends.
Inputs may be any that keep to these rules, and one draw needn't show every extreme that they name: Owner o holds span slot_span[o]; each span is held by exactly one owner. `span_place`: within each request every position 0 to 15 is taken by exactly one span. Spans 0, 1 and 16 stand at positions 0, 1 and 2 of request 0. `row_index`: within each span the entries are distinct and increasing. `block_count`: some span has 2 blocks and some has 1.
All inputs are finite; a program needn't handle non-finite values.
Results may differ from the reference program's by a relative error of at most 0.01.
The reference program's roundings to bfloat16 on the way count: a program that leaves them out, or rounds other values in their place, can miss the bound.
Values may be sent and summed in bfloat16 or wider, within the bound.
No kernel may reach another device: no remote copies, remote signals or barrier semaphores. Data moves between devices by JAX's collectives and lax.ppermute only.
A program may use at most 64 MiB of HBM per device.

```python
import math
import jax
import jax.numpy as jnp
from jax import lax

D = 8192
HD = 128
QH = 8
SPAN = 512
BLK = 128
NB = 2
ROWS = 256
KVH = 8
N_CTX = 32
N_HEAD = 8


def draw_queries(key, part):
    key = jax.random.fold_in(key, 11)
    first = jax.random.fold_in(key, 0)
    shape = (N_CTX * NB * BLK, N_HEAD * QH * HD)
    return jax.random.normal(first, shape, jnp.float32).astype(jnp.bfloat16)


def draw_span_place(key, part):
    key = jax.random.fold_in(key, 31)
    first, second = jax.random.split(key)
    half = N_CTX // 2
    quarter = N_CTX // 4
    rest = 3 + jax.random.permutation(first, half - 3)
    lead = jnp.array([0, 1], dtype=jnp.int32)
    mark = jnp.array([2], dtype=jnp.int32)
    request_zero = jnp.concatenate([lead, rest[:quarter - 2].astype(jnp.int32), mark, rest[quarter - 2:].astype(jnp.int32)])
    request_one = jax.random.permutation(second, half).astype(jnp.int32)
    stacked = jnp.stack([request_zero.reshape(quarter, 2), request_one.reshape(quarter, 2)], axis=1)
    return stacked.reshape(-1).astype(jnp.int32)


def draw_row_index(key, part):
    key = jax.random.fold_in(key, 41)
    score = jax.random.randint(key, (N_CTX, SPAN), 0, 2 ** 18) * SPAN + jnp.arange(SPAN, dtype=jnp.int32)[None, :]
    order = jnp.argsort(score, axis=1, stable=True)[:, :NB * BLK]
    return jnp.sort(order, axis=1).astype(jnp.int32)


def draw_block_count(key, part):
    key = jax.random.fold_in(key, 51)
    first, second, third = jax.random.split(key, 3)
    counts = jax.random.randint(first, (N_CTX,), 1, NB + 1)
    fullest = jax.random.randint(second, (), 0, N_CTX)
    emptiest = (fullest + jax.random.randint(third, (), 1, N_CTX)) % N_CTX
    span_ids = jnp.arange(N_CTX, dtype=jnp.int32)
    counts = jnp.where(span_ids == fullest, NB, counts)
    counts = jnp.where(span_ids == emptiest, 1, counts)
    return counts.astype(jnp.int32)


def shard_levels(own_key, shape, shards, low, high):
    gain = 1.0
    for axis_at, shards_of in shards:
        steps = jax.random.uniform(jax.random.fold_in(jax.random.fold_in(own_key, 6), axis_at), (shards_of,), jnp.float32, low / len(shards), high / len(shards))
        gain = gain * jnp.repeat(jnp.exp(steps), shape[axis_at] // shards_of).reshape((-1,) + (1,) * (len(shape) - 1 - axis_at))
    return gain


def centred(key, shape, deviation, limit, shards=(), kind=jnp.bfloat16):
    values = jax.random.normal(key, shape, jnp.float32) * deviation
    if len(shards) > 0:
        values = shard_levels(key, shape, shards, -0.22, 0.18) * values
    return jnp.clip(values, min=-limit, max=limit).astype(kind)


def setup_inputs(seed: int = 0) -> dict:
    key_list = jax.random.split(jax.random.key(seed), 9)
    hidden_rows = centred(key_list[0], (N_CTX * ROWS, D), 1.0, 6.0, ((0, 32), (1, 8)))
    kv_weight = centred(key_list[1], (D, KVH * 2 * HD), D ** -0.5, 0.0625, ((1, 8),))
    queries = draw_queries(jax.random.fold_in(key_list[8], 71), 0)
    kv_pool = centred(key_list[3], (N_CTX * SPAN, KVH * 2 * HD), 1.0, 6.0, ((0, 32), (1, 8)))
    slot_span = jax.random.permutation(key_list[4], N_CTX).astype(jnp.int32)
    span_place = draw_span_place(jax.random.fold_in(key_list[8], 71), 0)
    row_index = draw_row_index(jax.random.fold_in(key_list[8], 71), 0)
    block_count = draw_block_count(jax.random.fold_in(key_list[8], 71), 0)
    return {"hidden_rows": hidden_rows, "kv_weight": kv_weight, "queries": queries, "kv_pool": kv_pool, "slot_span": slot_span, "span_place": span_place, "row_index": row_index, "block_count": block_count}


def rope_freqs(size):
    half = size // 2
    base = 500000.0 ** (-2.0 * jnp.arange(half, dtype=jnp.float32) / size)
    wavelen = 2.0 * math.pi / base
    smooth = (8192.0 / wavelen - 1.0) / 3.0
    blended = (1.0 - smooth) * base / 8.0 + smooth * base
    return jnp.where(wavelen < 2048.0, base, jnp.where(wavelen > 8192.0, base / 8.0, blended))


def rotate_keys(keys, positions):
    half = keys.shape[-1] // 2
    freqs = rope_freqs(keys.shape[-1])
    angles = positions.astype(jnp.float32)[:, None] * freqs[None, :]
    angles = angles.reshape(angles.shape[:1] + (1,) * (keys.ndim - 2) + angles.shape[1:])
    cosine = jnp.cos(angles)
    sine = jnp.sin(angles)
    first = keys[..., :half]
    second = keys[..., half:]
    return jnp.concatenate([first * cosine - second * sine, second * cosine + first * sine], axis=-1)


def by_request(values, per_span):
    rest = values.shape[1:]
    quads = values.shape[0] // (4 * per_span)
    grouped = values.reshape((quads, 2, 2, per_span) + rest)
    grouped = jnp.swapaxes(grouped, 0, 1)
    return grouped.reshape((2, quads * 2 * per_span) + rest)


def reference(hidden_rows, kv_weight, queries, kv_pool, slot_span, span_place, row_index, block_count):
    groups = N_HEAD
    projected = jnp.dot(hidden_rows, kv_weight, preferred_element_type=jnp.float32)
    projected = projected.reshape(N_CTX * ROWS, groups, 2, HD)
    fresh_pos = (span_place[:, None] * SPAN + row_index).reshape(-1).astype(jnp.int32)
    fresh_keys = rotate_keys(projected[:, :, 0], fresh_pos).astype(jnp.bfloat16)
    fresh_vals = projected[:, :, 1].astype(jnp.bfloat16)
    fresh_kv = jnp.stack([fresh_keys, fresh_vals], axis=2).reshape(N_CTX * ROWS, groups * 2 * HD)
    span_ids = jnp.arange(N_CTX, dtype=jnp.int32)
    holder = jnp.sum(jnp.where(slot_span[None, :] == span_ids[:, None], span_ids[None, :], 0), axis=1).astype(jnp.int32)
    slots = kv_pool.reshape(N_CTX, SPAN, groups, 2, HD)
    cached = jnp.take(slots, holder, axis=0)
    offsets = jnp.repeat(span_place * SPAN, SPAN).astype(jnp.int32)
    cached_keys = rotate_keys(cached[:, :, :, 0].reshape(N_CTX * SPAN, groups, HD).astype(jnp.float32), offsets)
    cached_keys = cached_keys.astype(jnp.bfloat16)
    cached_vals = cached[:, :, :, 1].reshape(N_CTX * SPAN, groups, HD)
    live = jnp.arange(ROWS, dtype=jnp.int32)[None, :] < (block_count * BLK)[:, None]
    replaced = jnp.any((row_index[:, :, None] == jnp.arange(SPAN, dtype=jnp.int32)[None, None, :]) & live[:, :, None], axis=1)
    cached_pos = (span_place[:, None] * SPAN + jnp.arange(SPAN, dtype=jnp.int32)[None, :]).astype(jnp.int32)
    keys_all = jnp.concatenate([by_request(cached_keys, SPAN), by_request(fresh_keys, ROWS)], axis=1)
    vals_all = jnp.concatenate([by_request(cached_vals, SPAN), by_request(fresh_vals, ROWS)], axis=1)
    pos_all = jnp.concatenate([by_request(cached_pos.reshape(-1), SPAN), by_request(fresh_pos, ROWS)], axis=1)
    usable_all = jnp.concatenate([by_request(jnp.logical_not(replaced).reshape(-1), SPAN), by_request(live.reshape(-1), ROWS)], axis=1)
    query_blocks = queries.reshape(N_CTX, ROWS, groups, QH, HD)
    query_pos_all = fresh_pos.reshape(N_CTX, ROWS)
    scale = HD ** -0.5

    def one_span(index):
        request = (index // 2) % 2
        keys = lax.dynamic_index_in_dim(keys_all, request, 0, keepdims=False)
        vals = lax.dynamic_index_in_dim(vals_all, request, 0, keepdims=False)
        key_pos = lax.dynamic_index_in_dim(pos_all, request, 0, keepdims=False)
        usable = lax.dynamic_index_in_dim(usable_all, request, 0, keepdims=False)
        query_pos = lax.dynamic_index_in_dim(query_pos_all, index, 0, keepdims=False)
        query_live = lax.dynamic_index_in_dim(live, index, 0, keepdims=False)
        allowed = usable[None, :] & (key_pos[None, :] <= query_pos[:, None])
        allowed = allowed | jnp.logical_not(query_live)[:, None]
        block = lax.dynamic_index_in_dim(query_blocks, index, 0, keepdims=False)

        def one_group(operands):
            group_queries, group_keys, group_vals = operands
            scores = jnp.einsum("rqd,nd->rqn", group_queries.astype(jnp.float32), group_keys.astype(jnp.float32)) * scale
            masked = jnp.where(allowed[:, None, :], scores, -jnp.inf)
            largest = jnp.max(masked, axis=-1, keepdims=True)
            weights = jnp.where(allowed[:, None, :], jnp.exp(scores - largest), 0.0)
            total = jnp.sum(weights, axis=-1)
            rounded = lax.optimization_barrier(weights.astype(jnp.bfloat16))
            mixed = jnp.einsum("rqn,nd->rqd", rounded.astype(jnp.float32), group_vals.astype(jnp.float32))
            return mixed / total[..., None]

        result = lax.map(one_group, (block.transpose(1, 0, 2, 3), keys.transpose(1, 0, 2), vals.transpose(1, 0, 2)))
        result = result.transpose(1, 0, 2, 3)
        return jnp.where(query_live[:, None, None, None], result, 0.0)

    attended = lax.map(one_span, span_ids)
    attended = attended.reshape(N_CTX * ROWS, groups * QH * HD).astype(jnp.bfloat16)
    return fresh_kv, attended
```

```python
import functools
import math

import jax
import jax.numpy as jnp
import numpy as np
from jax import lax
from jax.experimental import pallas as pl
from jax.experimental.pallas import tpu as pltpu
from jax.sharding import PartitionSpec as P

BLK = 128
LANES = 256


def rope_freqs(size):
    half = size // 2
    base = 500000.0 ** (-2.0 * jnp.arange(half, dtype=jnp.float32) / size)
    wavelen = 2.0 * math.pi / base
    smooth = (8192.0 / wavelen - 1.0) / 3.0
    blended = (1.0 - smooth) * base / 8.0 + smooth * base
    return jnp.where(wavelen < 2048.0, base, jnp.where(wavelen > 8192.0, base / 8.0, blended))


def rope_table(positions, size):
    angles = positions.astype(jnp.float32)[:, None] * rope_freqs(size)[None, :]
    cosine, sine = jnp.cos(angles), jnp.sin(angles)
    return jnp.stack(
        [jnp.concatenate([cosine, cosine], 1), jnp.concatenate([-sine, sine], 1)], axis=1
    )


def rotate(keys, cosine, sine):
    return keys * cosine + pltpu.roll(keys, keys.shape[-1] // 2, 1) * sine


def project_kernel(hid_ref, weight_ref, turn_ref, out_ref, acc_ref):
    part = jnp.dot(hid_ref[0], weight_ref[...], preferred_element_type=jnp.float32)
    step = pl.program_id(0)

    @pl.when(step == 0)
    def _():
        acc_ref[...] = part

    @pl.when(step > 0)
    def _():
        acc_ref[...] += part

    @pl.when(step == pl.num_programs(0) - 1)
    def _():
        width = acc_ref.shape[1] // 2
        keys = rotate(acc_ref[:, :width], turn_ref[:, 0], turn_ref[:, 1])
        out_ref[:, :width] = keys.astype(out_ref.dtype)
        out_ref[:, width:] = acc_ref[:, width:].astype(out_ref.dtype)


def project(gathered, weight, turn):
    chunks, rows, depth = gathered.shape
    cols = weight.shape[1]
    return pl.pallas_call(
        project_kernel,
        grid=(chunks,),
        in_specs=[
            pl.BlockSpec((1, rows, depth), lambda i: (i, 0, 0)),
            pl.BlockSpec((depth, cols), lambda i: (i, 0)),
            pl.BlockSpec(turn.shape, lambda i: (0, 0, 0)),
        ],
        out_specs=pl.BlockSpec((rows, cols), lambda i: (0, 0)),
        out_shape=jax.ShapeDtypeStruct((rows, cols), jnp.bfloat16),
        scratch_shapes=[pltpu.VMEM((rows, cols), jnp.float32)],
        name="project",
    )(gathered, weight, turn)


def attend_kernel(
    slot_ref,
    place_ref,
    count_ref,
    me_ref,
    q_ref,
    rows_ref,
    turn_ref,
    pool_ref,
    fresh_ref,
    out_ref,
    by_place,
    owner_of,
    pool_buf,
    fresh_buf,
    q_scr,
    k_scr,
    v_scr,
    acc_scr,
    max_scr,
    sum_scr,
    sems,
):
    spans, rows = rows_ref.shape
    span_len = pool_buf.shape[1]
    width = pool_buf.shape[2] // 2
    heads = q_ref.shape[1] // width
    per = LANES // BLK
    tiles_per_block = heads // per
    log2e = 1.4426950408889634
    factor = width**-0.5 * log2e
    me = me_ref[0]
    mine = (me // 2) % 2
    my_place = place_ref[me]
    my_blocks = count_ref[me]
    n_tiles = my_blocks * tiles_per_block

    def fill(s, carry):
        owner_of[slot_ref[s]] = s

        @pl.when((s // 2) % 2 == mine)
        def _():
            by_place[place_ref[s]] = s

        return carry

    lax.fori_loop(0, spans, fill, 0)

    def at_step(i):
        return by_place[jnp.where(i == 0, my_place, i - 1)]

    def copies(i, slot):
        span = at_step(i)
        return (
            pltpu.make_async_copy(
                pool_ref.at[owner_of[span]], pool_buf.at[slot], sems.at[0, slot]
            ),
            pltpu.make_async_copy(
                fresh_ref.at[(span // 4) * 2 + span % 2], fresh_buf.at[slot], sems.at[1, slot]
            ),
        )

    for c in copies(0, 0):
        c.start()

    for b in range(rows // BLK):
        for h in range(heads):
            piece = q_ref[b * BLK : (b + 1) * BLK, h * width : (h + 1) * width]
            j = b * tiles_per_block + h // per
            lo = (h % per) * BLK
            q_scr[j, :, lo : lo + BLK] = piece.T

    def prepare(i, slot):
        span = at_step(i)
        place = place_ref[span]
        live = count_ref[span] * BLK
        picks = rows_ref[pl.ds(span, 1), :]
        picks = jnp.where(lax.broadcasted_iota(jnp.int32, (1, rows), 1) < live, picks, -1)
        here = lax.broadcasted_iota(jnp.int32, (span_len, rows), 0)
        chosen = (here == picks).astype(jnp.float32)
        replaced = jnp.sum(chosen, axis=1, keepdims=True) > 0.5
        chosen = chosen.astype(jnp.bfloat16)
        moved = jnp.dot(chosen, fresh_buf[slot], preferred_element_type=jnp.float32)
        cached = pool_buf[slot].astype(jnp.float32)
        turn = turn_ref[place]
        keys = rotate(cached[:, :width], turn[0:1], turn[1:2])
        k_scr[...] = jnp.where(replaced, moved[:, :width], keys).astype(jnp.bfloat16)
        vals = jnp.where(replaced, moved[:, width:], cached[:, width:])
        v_scr[...] = vals.T.astype(jnp.bfloat16)

    def step(i, diagonal):
        slot = lax.rem(i, 2)

        @pl.when(i < my_place)
        def _():
            for c in copies(i + 1, 1 - slot):
                c.start()

        for c in copies(i, slot):
            c.wait()
        prepare(i, slot)

        def tile(j, carry):
            scores = jnp.dot(k_scr[...], q_scr[j], preferred_element_type=jnp.float32)
            if diagonal:
                block = j // tiles_per_block
                limit = rows_ref[pl.ds(me, 1), :]
                limit = jnp.where(block == 0, limit[:, :BLK], limit[:, BLK:])
                limit = jnp.concatenate([limit] * per, axis=1)
                here = lax.broadcasted_iota(jnp.int32, scores.shape, 0)
                scores = jnp.where(here <= limit, scores, -1e30)
                largest = jnp.max(scores, axis=0, keepdims=True)
            else:
                old = max_scr[j]
                largest = jnp.maximum(old, jnp.max(scores, axis=0, keepdims=True))
            weights = jnp.exp2((scores - largest) * factor)
            total = jnp.sum(weights, axis=0, keepdims=True)
            mixed = jnp.dot(
                v_scr[...], weights.astype(jnp.bfloat16), preferred_element_type=jnp.float32
            )
            if diagonal:
                sum_scr[j] = total
                acc_scr[j] = mixed
            else:
                shrink = jnp.exp2((old - largest) * factor)
                sum_scr[j] = sum_scr[j] * shrink + total
                acc_scr[j] = acc_scr[j] * shrink + mixed
            max_scr[j] = largest
            return carry

        def group(g, carry):
            for k in range(tiles_per_block):
                tile(g * tiles_per_block + k, 0)
            return carry

        lax.fori_loop(0, my_blocks, group, 0)

    step(0, True)

    def rest(i, carry):
        step(i, False)
        return carry

    lax.fori_loop(1, my_place + 1, rest, 0)

    for b in range(rows // BLK):

        @pl.when(b < my_blocks)
        def _():
            for h in range(heads):
                j = b * tiles_per_block + h // per
                lo = (h % per) * BLK
                piece = acc_scr[j, :, lo : lo + BLK] / sum_scr[j, :, lo : lo + BLK]
                out_ref[b * BLK : (b + 1) * BLK, h * width : (h + 1) * width] = piece.T.astype(
                    out_ref.dtype
                )

        @pl.when(b >= my_blocks)
        def _():
            out_ref[b * BLK : (b + 1) * BLK, :] = jnp.zeros(
                (BLK, heads * width), out_ref.dtype
            )


def attend(slot_span, span_place, block_count, me, queries, row_index, turn, pool, fresh):
    spans, span_len, both = pool.shape
    rows = fresh.shape[1]
    width = both // 2
    heads = queries.shape[1] // width
    tiles = rows * heads // LANES
    smem = pl.BlockSpec(memory_space=pltpu.SMEM)
    vmem = pl.BlockSpec(memory_space=pltpu.VMEM)
    hbm = pl.BlockSpec(memory_space=pl.ANY)
    return pl.pallas_call(
        attend_kernel,
        in_specs=[smem, smem, smem, smem, vmem, vmem, vmem, hbm, hbm],
        out_specs=vmem,
        out_shape=jax.ShapeDtypeStruct(queries.shape, queries.dtype),
        scratch_shapes=[
            pltpu.SMEM((spans,), jnp.int32),
            pltpu.SMEM((spans,), jnp.int32),
            pltpu.VMEM((2, span_len, both), jnp.bfloat16),
            pltpu.VMEM((2, rows, both), jnp.bfloat16),
            pltpu.VMEM((tiles, width, LANES), jnp.bfloat16),
            pltpu.VMEM((span_len, width), jnp.bfloat16),
            pltpu.VMEM((width, span_len), jnp.bfloat16),
            pltpu.VMEM((tiles, width, LANES), jnp.float32),
            pltpu.VMEM((tiles, 1, LANES), jnp.float32),
            pltpu.VMEM((tiles, 1, LANES), jnp.float32),
            pltpu.SemaphoreType.DMA((2, 2)),
        ],
        compiler_params=pltpu.CompilerParams(vmem_limit_bytes=40 * 1024 * 1024),
        name="attend",
    )(slot_span, span_place, block_count, me, queries, row_index, turn, pool, fresh)


def shards(hidden_rows, kv_weight, queries, kv_pool, slot_span, span_place, row_index, block_count):
    width = kv_weight.shape[1] // 2
    span_len = kv_pool.shape[0]
    spans = span_place.shape[0]
    position = lax.axis_index("ctx")
    my_pos = span_place[position] * span_len + lax.dynamic_index_in_dim(
        row_index, position, 0, keepdims=False
    )
    groups = [[c for c in range(spans) if c // 2 % 2 == q] for q in range(2)]
    gathered = lax.all_gather(hidden_rows, "head", axis=0)
    fresh = project(gathered, kv_weight, rope_table(my_pos, width))
    all_fresh = lax.all_gather(fresh, "ctx", axis=0, axis_index_groups=groups)
    all_pool = lax.all_gather(kv_pool, "ctx", axis=0)
    turn = rope_table(jnp.arange(spans // 2, dtype=jnp.int32) * span_len, width)
    attended = attend(
        slot_span,
        span_place,
        block_count,
        position.astype(jnp.int32).reshape(1),
        queries,
        row_index,
        turn,
        all_pool,
        all_fresh,
    )
    return fresh, attended


def solution(mesh):
    in_specs = (
        P("ctx", "head"),
        P(None, "head"),
        P("ctx", "head"),
        P("ctx", "head"),
        P(),
        P(),
        P(),
        P(),
    )
    out_specs = (P("ctx", "head"), P("ctx", "head"))
    return jax.shard_map(shards, mesh=mesh, in_specs=in_specs, out_specs=out_specs, check_vma=False)
```

```python
import functools
import math

import jax
import jax.numpy as jnp
import numpy as np
from jax import lax
from jax.experimental import pallas as pl
from jax.experimental.pallas import tpu as pltpu
from jax.sharding import PartitionSpec as P

BLK = 128
LANES = 256
NX = 4
NZ = 8
NY = 4
KEEP = 3
LOG2E = 1.4426950408889634

SMEM = pl.BlockSpec(memory_space=pltpu.SMEM)
VMEM = pl.BlockSpec(memory_space=pltpu.VMEM)
HBM = pl.BlockSpec(memory_space=pl.ANY)


def rope_freqs(size):
    half = size // 2
    base = 500000.0 ** (-2.0 * jnp.arange(half, dtype=jnp.float32) / size)
    wavelen = 2.0 * math.pi / base
    smooth = (8192.0 / wavelen - 1.0) / 3.0
    blended = (1.0 - smooth) * base / 8.0 + smooth * base
    return jnp.where(wavelen < 2048.0, base, jnp.where(wavelen > 8192.0, base / 8.0, blended))


def rope_table(positions, size):
    angles = positions.astype(jnp.float32)[:, None] * rope_freqs(size)[None, :]
    cosine, sine = jnp.cos(angles), jnp.sin(angles)
    return jnp.stack(
        [jnp.concatenate([cosine, cosine], 1), jnp.concatenate([-sine, sine], 1)], axis=1
    )


def place_table(places, span_len, size):
    half = size // 2
    base = 500000.0 ** (-2.0 * np.arange(half) / size)
    wavelen = 2.0 * math.pi / base
    smooth = (8192.0 / wavelen - 1.0) / 3.0
    blended = (1.0 - smooth) * base / 8.0 + smooth * base
    freqs = np.where(wavelen < 2048.0, base, np.where(wavelen > 8192.0, base / 8.0, blended))
    positions = np.arange(places, dtype=np.float32) * span_len
    angles = (positions[:, None] * freqs.astype(np.float32)[None, :]).astype(np.float64)
    cosine, sine = np.cos(angles), np.sin(angles)
    table = np.stack([np.concatenate([cosine, cosine], 1), np.concatenate([-sine, sine], 1)], 1)
    return table.astype(np.float32)


def rotate(keys, cosine, sine):
    return keys * cosine + pltpu.roll(keys, keys.shape[-1] // 2, 1) * sine


def contract_first(a, b):
    return lax.dot_general(a, b, (((0,), (0,)), ((), ())), preferred_element_type=jnp.float32)


def compact_kernel(slot_ref, place_ref, count_ref, me_ref, rows_ref, turn_ref, pool_ref, both_ref, keys_ref):
    span_len = pool_ref.shape[0]
    width = pool_ref.shape[1] // 2
    rows = rows_ref.shape[1]
    span = slot_ref[me_ref[0]]
    live = count_ref[span] * BLK
    picks = rows_ref[pl.ds(span, 1), :]
    lane = lax.broadcasted_iota(jnp.int32, (1, rows), 1)
    picks = jnp.where(lane < live, picks, 4 * span_len)
    here = lax.broadcasted_iota(jnp.int32, (span_len, rows), 0)
    before = jnp.sum((picks < here).astype(jnp.float32), axis=1, keepdims=True)
    gone = jnp.sum((picks == here).astype(jnp.float32), axis=1, keepdims=True)
    row = lax.broadcasted_iota(jnp.int32, (span_len, 1), 0)
    rank = jnp.where(gone > 0.5, -1, row - before.astype(jnp.int32))
    target = lax.broadcasted_iota(jnp.int32, (span_len, KEEP * BLK), 1)
    chosen = jnp.where(rank == target, 1.0, 0.0).astype(jnp.bfloat16)
    turn = turn_ref[place_ref[span]]
    keys = rotate(pool_ref[:, :width].astype(jnp.float32), turn[0:1], turn[1:2])
    kept = contract_first(chosen, keys.astype(jnp.bfloat16)).astype(jnp.bfloat16)
    vals = contract_first(pool_ref[:, width:], chosen).astype(jnp.bfloat16)
    for i in range(KEEP):
        both_ref[i] = kept[i * BLK : (i + 1) * BLK]
        keys_ref[i] = kept[i * BLK : (i + 1) * BLK]
        both_ref[KEEP + i] = vals[:, i * BLK : (i + 1) * BLK]


def compact(slot_span, span_place, block_count, me, row_index, turn, pool):
    return pl.pallas_call(
        compact_kernel,
        in_specs=[SMEM, SMEM, SMEM, SMEM, VMEM, VMEM, VMEM],
        out_specs=(VMEM, VMEM),
        out_shape=(
            jax.ShapeDtypeStruct((2 * KEEP, BLK, BLK), pool.dtype),
            jax.ShapeDtypeStruct((KEEP, BLK, BLK), pool.dtype),
        ),
        name="compact",
    )(slot_span, span_place, block_count, me, row_index, turn, pool)


def head_of(me_ref, step, sibling):
    head = me_ref[1]
    core = head % 2
    return ((head // 2 + step) % NY) * 2 + (1 - core if sibling else core)


def load_weight(me_ref, weight_ref, buf, sems, which):
    depth = buf.shape[1]
    copies = []
    for i, (step, sibling) in enumerate(which):
        first = pl.multiple_of(head_of(me_ref, step, sibling) * depth, depth)
        copy = pltpu.make_async_copy(weight_ref.at[pl.ds(first, depth)], buf.at[i], sems.at[i])
        copy.start()
        copies.append(copy)
    return copies


FIRST = ((0, False), (0, True), (-1, False), (-1, True), (1, False), (1, True))
LAST = ((2, False), (2, True))


def project_first_kernel(me_ref, *refs):
    n = len(FIRST)
    hid, weight_ref, out_ref, buf, sems = refs[:n], refs[n], refs[n + 1], refs[n + 2], refs[n + 3]
    copies = load_weight(me_ref, weight_ref, buf, sems, FIRST)
    total = None
    for i in range(n):
        copies[i].wait()
        part = jnp.dot(hid[i][...], buf[i], preferred_element_type=jnp.float32)
        total = part if total is None else total + part
    out_ref[...] = total


def project_last_kernel(me_ref, *refs):
    hid, weight_ref, partial_ref, turn_ref = refs[:4], refs[4], refs[5], refs[6]
    out_ref, chunk_ref, buf, sems = refs[7:]
    rows = out_ref.shape[0]
    width = out_ref.shape[1] // 2
    copies = load_weight(me_ref, weight_ref, buf, sems, LAST)
    for c in copies:
        c.wait()
    half = rows // 2
    for b in range(2):
        at = slice(b * half, (b + 1) * half)
        total = partial_ref[at]
        for i in range(2):
            total += jnp.dot(hid[2 * i + b][...], buf[i], preferred_element_type=jnp.float32)
        keys = rotate(total[:, :width], turn_ref[at, 0], turn_ref[at, 1]).astype(out_ref.dtype)
        out_ref[at, :width] = keys
        out_ref[at, width:] = total[:, width:].astype(out_ref.dtype)
        chunk_ref[b] = keys
        chunk_ref[2 + b] = total[:, width:].T.astype(out_ref.dtype)


def project(me, hidden, weight, turn):
    first, last = hidden
    rows, depth = first[0].shape
    cols = weight.shape[1]
    partial = pl.pallas_call(
        project_first_kernel,
        in_specs=[SMEM] + [VMEM] * len(FIRST) + [HBM],
        out_specs=VMEM,
        out_shape=jax.ShapeDtypeStruct((rows, cols), jnp.float32),
        scratch_shapes=[
            pltpu.VMEM((len(FIRST), depth, cols), weight.dtype),
            pltpu.SemaphoreType.DMA((len(FIRST),)),
        ],
        compiler_params=pltpu.CompilerParams(vmem_limit_bytes=24 * 1024 * 1024),
        name="project_first",
    )(me, *first, weight)
    return pl.pallas_call(
        project_last_kernel,
        in_specs=[SMEM] + [VMEM] * 4 + [HBM, VMEM, VMEM],
        out_specs=(VMEM, VMEM),
        out_shape=(
            jax.ShapeDtypeStruct((rows, cols), weight.dtype),
            jax.ShapeDtypeStruct((4, BLK, BLK), weight.dtype),
        ),
        scratch_shapes=[
            pltpu.VMEM((len(LAST), depth, cols), weight.dtype),
            pltpu.SemaphoreType.DMA((len(LAST),)),
        ],
        name="project_last",
    )(me, *last, weight, partial, turn)


class Scan:
    def __init__(self, q_scr, acc_scr, max_scr, sum_scr, blocks, per_block, factor):
        self.q, self.acc, self.max, self.sum = q_scr, acc_scr, max_scr, sum_scr
        self.blocks, self.per_block, self.factor = blocks, per_block, factor

    def tile(self, j, keys, vals, mask, first):
        scores = jnp.dot(keys, self.q[j], preferred_element_type=jnp.float32)
        if mask is not None:
            seen = mask(j // self.per_block, scores.shape)
            scores = jnp.where(seen, scores, -1e30)
        largest = jnp.max(scores, axis=0, keepdims=True)
        if not first:
            old = self.max[j]
            largest = jnp.maximum(old, largest)
        weights = jnp.exp2((scores - largest) * self.factor)
        if mask is not None:
            weights = jnp.where(seen, weights, 0.0)
        total = jnp.sum(weights, axis=0, keepdims=True)
        mixed = jnp.dot(vals, weights.astype(jnp.bfloat16), preferred_element_type=jnp.float32)
        if not first:
            shrink = jnp.exp2((old - largest) * self.factor)
            total = self.sum[j] * shrink + total
            mixed = self.acc[j] * shrink + mixed
        self.max[j] = largest
        self.sum[j] = total
        self.acc[j] = mixed

    def step(self, keys, vals, mask=None, first=False):
        keys = keys[0] if len(keys) == 1 else jnp.concatenate(keys, axis=0)
        vals = vals[0] if len(vals) == 1 else jnp.concatenate(vals, axis=1)

        def block(b, carry):
            for k in range(self.per_block):
                self.tile(b * self.per_block + k, keys, vals, mask, first)
            return carry

        lax.fori_loop(0, self.blocks, block, 0)

    def chunks(self, list_ref, count, fetch):
        group = 4

        def many(g, carry):
            got = [fetch(list_ref[g * group + i]) for i in range(group)]
            self.step([k for k, _ in got], [v for _, v in got])
            return carry

        lax.fori_loop(0, count // group, many, 0)

        def one(i, carry):
            key, val = fetch(list_ref[i])
            self.step([key], [val])
            return carry

        lax.fori_loop(count // group * group, count, one, 0)


def tables(slot_ref, place_ref, mine, by_place, owner_of):
    def fill(s, carry):
        owner_of[slot_ref[s]] = s

        @pl.when((s // 2) % 2 == mine)
        def _():
            by_place[place_ref[s]] = s

        return carry

    lax.fori_loop(0, slot_ref.shape[0], fill, 0)


def make_list(list_ref, my_place, chunks_of):
    def add(p, count):
        base, number = chunks_of(p)

        def put(i, carry):
            list_ref[count + i] = base + i
            return carry

        lax.fori_loop(0, number, put, 0)
        return count + number

    return lax.fori_loop(0, my_place, add, 0)


def limits(rows_ref, me, block, per, minus):
    row = rows_ref[pl.ds(me, 1), :]
    if minus:
        row = row - lax.broadcasted_iota(jnp.int32, row.shape, 1)
    row = jnp.where(block == 0, row[:, :BLK], row[:, BLK:])
    return jnp.concatenate([row] * per, axis=1)


SECTION = (0, 1, 7, 2, 6)
REST = (3, 5, 4)


def cached_kernel(slot_ref, place_ref, count_ref, me_ref, q_ref, rows_ref, *refs):
    own, more, sec, rest = refs[:NZ], refs[NZ : 2 * NZ], refs[2 * NZ : 2 * NZ + 3], refs[2 * NZ + 3 : 2 * NZ + 6]
    q_scr, acc_scr, max_scr, sum_scr = refs[2 * NZ + 6 : 2 * NZ + 10]
    by_place, owner_of, list_ref, kbuf, vbuf, sems = refs[2 * NZ + 10 :]
    width = BLK
    rows = q_ref.shape[0]
    heads = q_ref.shape[1] // width
    per = LANES // BLK
    per_block = heads // per
    me = me_ref[0]
    my_place = place_ref[me]
    copies = []

    def bring(source, target, n):
        copy = pltpu.make_async_copy(source, target, sems.at[len(copies)])
        copy.start()
        copies.append(copy)

    for d in range(NZ):
        bring(own[d].at[pl.ds(0, KEEP)], kbuf.at[pl.ds(d * KEEP, KEEP)], KEEP)
        bring(own[d].at[pl.ds(KEEP, KEEP)], vbuf.at[pl.ds(d * KEEP, KEEP)], KEEP)
        for e in range(1, NX):
            at = pl.ds((e * NZ + d) * KEEP, KEEP)
            bring(more[d].at[pl.ds((e - 1) * KEEP, KEEP)], kbuf.at[at], KEEP)
            if d in SECTION:
                bring(sec[e - 1].at[pl.ds(SECTION.index(d) * KEEP, KEEP)], vbuf.at[at], KEEP)
            else:
                bring(rest[e - 1].at[pl.ds(REST.index(d) * KEEP, KEEP)], vbuf.at[at], KEEP)

    tables(slot_ref, place_ref, (me // 2) % 2, by_place, owner_of)

    def where_is(span):
        owner = owner_of[span]
        d = (owner // NX - me // NX + NZ) % NZ
        e = (owner % NX - me % NX + NX) % NX
        return (e * NZ + d) * KEEP, 4 - count_ref[span]

    count = make_list(list_ref, my_place, lambda p: where_is(by_place[p]))
    for b in range(rows // BLK):
        for h in range(heads):
            piece = q_ref[b * BLK : (b + 1) * BLK, h * width : (h + 1) * width]
            lo = (h % per) * BLK
            q_scr[b * per_block + h // per, :, lo : lo + BLK] = piece.T
    for c in copies:
        c.wait()
    scan = Scan(q_scr, acc_scr, max_scr, sum_scr, count_ref[me], per_block, width**-0.5 * LOG2E)
    base, _ = where_is(me)

    def mask(block, shape):
        return lax.broadcasted_iota(jnp.int32, shape, 0) < limits(rows_ref, me, block, per, True)

    scan.step(
        [kbuf[base + i] for i in range(KEEP)], [vbuf[base + i] for i in range(KEEP)], mask, True
    )
    scan.chunks(list_ref, count, lambda c: (kbuf[c], vbuf[c]))


def fresh_kernel(slot_ref, place_ref, count_ref, me_ref, rows_ref, q_scr, acc_in, max_in, sum_in, *refs):
    own, pair = refs[:NZ], refs[NZ : 2 * NZ]
    out_ref = refs[2 * NZ]
    by_place, owner_of, list_ref, buf, acc_scr, max_scr, sum_scr, sems = refs[2 * NZ + 1 :]
    width = BLK
    rows = out_ref.shape[0]
    heads = out_ref.shape[1] // width
    per = LANES // BLK
    per_block = heads // per
    me = me_ref[0]
    my_place = place_ref[me]
    copies = []
    for d in range(NZ):
        for e, side in enumerate((own, pair)):
            n = len(copies)
            if isinstance(side[d], tuple):
                continue
            copy = pltpu.make_async_copy(side[d], buf.at[pl.ds((e * NZ + d) * 4, 4)], sems.at[n])
            copy.start()
            copies.append(copy)
    tables(slot_ref, place_ref, (me // 2) % 2, by_place, owner_of)

    def where_is(span):
        d = (span // NX - me // NX + NZ) % NZ
        e = jnp.where(span % NX == me % NX, 0, 1)
        return (e * NZ + d) * 4, count_ref[span]

    count = make_list(list_ref, my_place, lambda p: where_is(by_place[p]))
    acc_scr[...] = acc_in[...]
    max_scr[...] = max_in[...]
    sum_scr[...] = sum_in[...]
    for c in copies:
        c.wait()
    my_blocks = count_ref[me]
    scan = Scan(q_scr, acc_scr, max_scr, sum_scr, my_blocks, per_block, width**-0.5 * LOG2E)

    def mask(block, shape):
        lane = lax.broadcasted_iota(jnp.int32, shape, 1) % BLK
        return lax.broadcasted_iota(jnp.int32, shape, 0) <= block * BLK + lane

    scan.step([buf[0], buf[1]], [buf[2], buf[3]], mask)
    scan.chunks(list_ref, count, lambda c: (buf[c], buf[c + 2]))
    for b in range(rows // BLK):

        @pl.when(b < my_blocks)
        def _():
            for h in range(heads):
                j = b * per_block + h // per
                lo = (h % per) * BLK
                piece = acc_scr[j, :, lo : lo + BLK] / sum_scr[j, :, lo : lo + BLK]
                out_ref[b * BLK : (b + 1) * BLK, h * width : (h + 1) * width] = piece.T.astype(
                    out_ref.dtype
                )

        @pl.when(b >= my_blocks)
        def _():
            out_ref[b * BLK : (b + 1) * BLK, :] = jnp.zeros((BLK, heads * width), out_ref.dtype)


def attend_cached(slot_span, span_place, block_count, me, queries, row_index, own, more, sec, rest):
    spans = slot_span.shape[0]
    tiles = queries.shape[0] * queries.shape[1] // BLK // LANES
    n_copies = NZ * (2 + 2 * (NX - 1))
    return pl.pallas_call(
        cached_kernel,
        in_specs=[SMEM] * 4 + [VMEM] * 2 + [HBM] * (2 * NZ + 6),
        out_specs=(VMEM,) * 4,
        out_shape=(
            jax.ShapeDtypeStruct((tiles, BLK, LANES), queries.dtype),
            jax.ShapeDtypeStruct((tiles, BLK, LANES), jnp.float32),
            jax.ShapeDtypeStruct((tiles, 1, LANES), jnp.float32),
            jax.ShapeDtypeStruct((tiles, 1, LANES), jnp.float32),
        ),
        scratch_shapes=[
            pltpu.SMEM((spans,), jnp.int32),
            pltpu.SMEM((spans,), jnp.int32),
            pltpu.SMEM((spans * KEEP,), jnp.int32),
            pltpu.VMEM((spans * KEEP, BLK, BLK), queries.dtype),
            pltpu.VMEM((spans * KEEP, BLK, BLK), queries.dtype),
            pltpu.SemaphoreType.DMA((n_copies,)),
        ],
        compiler_params=pltpu.CompilerParams(vmem_limit_bytes=40 * 1024 * 1024),
        name="attend_cached",
    )(slot_span, span_place, block_count, me, queries, row_index, *own, *more, *sec, *rest)


def attend_fresh(slot_span, span_place, block_count, me, row_index, state, shape, own, pair):
    spans = slot_span.shape[0]
    q_t, acc, largest, total = state
    return pl.pallas_call(
        fresh_kernel,
        in_specs=[SMEM] * 4 + [VMEM] * 5 + [HBM] * (2 * NZ),
        out_specs=VMEM,
        out_shape=jax.ShapeDtypeStruct(shape, q_t.dtype),
        scratch_shapes=[
            pltpu.SMEM((spans,), jnp.int32),
            pltpu.SMEM((spans,), jnp.int32),
            pltpu.SMEM((spans * 2,), jnp.int32),
            pltpu.VMEM((2 * NZ * 4, BLK, BLK), q_t.dtype),
            pltpu.VMEM(acc.shape, jnp.float32),
            pltpu.VMEM(largest.shape, jnp.float32),
            pltpu.VMEM(total.shape, jnp.float32),
            pltpu.SemaphoreType.DMA((2 * NZ,)),
        ],
        compiler_params=pltpu.CompilerParams(vmem_limit_bytes=40 * 1024 * 1024),
        name="attend_fresh",
    )(slot_span, span_place, block_count, me, row_index, q_t, acc, largest, total, *own, *pair)


def shift_ctx(values, dz, dx):
    pairs = [
        (((z + dz) % NZ) * NX + (x + dx) % NX, z * NX + x) for z in range(NZ) for x in range(NX)
    ]
    return lax.ppermute(values, "ctx", pairs)


def swap_ctx(values):
    pairs = [(z * NX + (x ^ 1), z * NX + x) for z in range(NZ) for x in range(NX)]
    return lax.ppermute(values, "ctx", pairs)


def shift_head(values, dy):
    pairs = [(((y + dy) % NY) * 2 + c, y * 2 + c) for y in range(NY) for c in range(2)]
    return lax.ppermute(values, "head", pairs)


def swap_core(values):
    pairs = [(y * 2 + 1 - c, y * 2 + c) for y in range(NY) for c in range(2)]
    return lax.ppermute(values, "head", pairs)


def gather_hidden(hidden):
    half = hidden.shape[0] // 2
    low = shift_head(hidden, -1)
    high = shift_head(hidden, 1)
    far_top = shift_head(low[:half], -1)
    far_bottom = shift_head(high[half:], 1)
    first = (hidden, swap_core(hidden), low, swap_core(low), high, swap_core(high))
    last = (far_top, far_bottom, swap_core(far_top), swap_core(far_bottom))
    return first, last


def ring(values, up):
    got = [values] + [None] * (NZ - 1)
    for d in range(1, NZ // 2):
        got[d] = shift_ctx(got[d - 1], 1, 0)
        got[NZ - d] = shift_ctx(got[(NZ - d + 1) % NZ], -1, 0)
    if up:
        got[NZ // 2] = shift_ctx(got[NZ // 2 - 1], 1, 0)
    else:
        got[NZ // 2] = shift_ctx(got[NZ // 2 + 1], -1, 0)
    return got


def gather_pool(both, keys):
    own = ring(both, True)
    side = [shift_ctx(keys, 0, e) for e in (1, 2, 3)]
    more = ring(jnp.concatenate(side, axis=0), False)
    vals = [jnp.concatenate([own[d][KEEP:] for d in part], axis=0) for part in (SECTION, REST)]
    near = [[shift_ctx(v, 0, 1), shift_ctx(v, 0, -1)] for v in vals]
    sec = (near[0][0], shift_ctx(near[0][0], 0, 1), near[0][1])
    rest = (near[1][0], shift_ctx(near[1][1], 0, -1), near[1][1])
    return own, more, sec, rest


def gather_fresh(chunks):
    own = ring(chunks, True)
    return own, [swap_ctx(c) for c in own]


def shards(hidden_rows, kv_weight, queries, kv_pool, slot_span, span_place, row_index, block_count):
    width = kv_weight.shape[1] // 2
    span_len = kv_pool.shape[0]
    spans = span_place.shape[0]
    position = lax.axis_index("ctx")
    me = jnp.stack([position, lax.axis_index("head")]).astype(jnp.int32)
    my_pos = span_place[position] * span_len + lax.dynamic_index_in_dim(
        row_index, position, 0, keepdims=False
    )
    turn = jnp.asarray(place_table(spans // 2, span_len, width))
    both, keys = compact(slot_span, span_place, block_count, me, row_index, turn, kv_pool)
    hidden = gather_hidden(hidden_rows)
    own, more, sec, rest = gather_pool(both, keys)
    fresh, chunks = project(me, hidden, kv_weight, rope_table(my_pos, width))
    fresh_own, fresh_pair = gather_fresh(chunks)
    state = attend_cached(
        slot_span, span_place, block_count, me, queries, row_index, own, more, sec, rest
    )
    attended = attend_fresh(
        slot_span, span_place, block_count, me, row_index, state, queries.shape, fresh_own, fresh_pair
    )
    return fresh, attended


def solution(mesh):
    in_specs = (
        P("ctx", "head"),
        P(None, "head"),
        P("ctx", "head"),
        P("ctx", "head"),
        P(),
        P(),
        P(),
        P(),
    )
    out_specs = (P("ctx", "head"), P("ctx", "head"))
    return jax.shard_map(shards, mesh=mesh, in_specs=in_specs, out_specs=out_specs, check_vma=False)
```

```python
import math

import jax
import jax.numpy as jnp
import numpy as np
from jax import lax
from jax.experimental import pallas as pl
from jax.experimental.pallas import tpu as pltpu
from jax.sharding import PartitionSpec as P

BLK = 128
LANES = 128
NX = 4
NZ = 8
NY = 4
KEEP = 3
LOG2E = 1.4426950408889634

SMEM = pl.BlockSpec(memory_space=pltpu.SMEM)
VMEM = pl.BlockSpec(memory_space=pltpu.VMEM)
HBM = pl.BlockSpec(memory_space=pl.ANY)


def rope_freqs(size):
    half = size // 2
    base = 500000.0 ** (-2.0 * jnp.arange(half, dtype=jnp.float32) / size)
    wavelen = 2.0 * math.pi / base
    smooth = (8192.0 / wavelen - 1.0) / 3.0
    blended = (1.0 - smooth) * base / 8.0 + smooth * base
    return jnp.where(wavelen < 2048.0, base, jnp.where(wavelen > 8192.0, base / 8.0, blended))


def rope_table(positions, size):
    angles = positions.astype(jnp.float32)[:, None] * rope_freqs(size)[None, :]
    cosine, sine = jnp.cos(angles), jnp.sin(angles)
    return jnp.stack(
        [jnp.concatenate([cosine, cosine], 1), jnp.concatenate([-sine, sine], 1)], axis=1
    )


def place_table(places, span_len, size):
    half = size // 2
    base = 500000.0 ** (-2.0 * np.arange(half) / size)
    wavelen = 2.0 * math.pi / base
    smooth = (8192.0 / wavelen - 1.0) / 3.0
    blended = (1.0 - smooth) * base / 8.0 + smooth * base
    freqs = np.where(wavelen < 2048.0, base, np.where(wavelen > 8192.0, base / 8.0, blended))
    positions = np.arange(places, dtype=np.float32) * span_len
    angles = (positions[:, None] * freqs.astype(np.float32)[None, :]).astype(np.float64)
    cosine, sine = np.cos(angles), np.sin(angles)
    table = np.stack([np.concatenate([cosine, cosine], 1), np.concatenate([-sine, sine], 1)], 1)
    return table.astype(np.float32)


def rotate(keys, cosine, sine):
    return keys * cosine + pltpu.roll(keys, keys.shape[-1] // 2, 1) * sine


def contract_first(a, b):
    return lax.dot_general(a, b, (((0,), (0,)), ((), ())), preferred_element_type=jnp.float32)


def compact_kernel(slot_ref, place_ref, count_ref, me_ref, rows_ref, turn_ref, pool_ref, keys_ref, vals_ref):
    span_len = pool_ref.shape[0]
    width = pool_ref.shape[1] // 2
    rows = rows_ref.shape[1]
    span = slot_ref[me_ref[0]]
    live = count_ref[span] * BLK
    picks = rows_ref[pl.ds(span, 1), :]
    lane = lax.broadcasted_iota(jnp.int32, (1, rows), 1)
    picks = jnp.where(lane < live, picks, 4 * span_len)
    here = lax.broadcasted_iota(jnp.int32, (span_len, rows), 0)
    before = jnp.sum((picks < here).astype(jnp.float32), axis=1, keepdims=True)
    gone = jnp.sum((picks == here).astype(jnp.float32), axis=1, keepdims=True)
    row = lax.broadcasted_iota(jnp.int32, (span_len, 1), 0)
    rank = jnp.where(gone > 0.5, -1, row - before.astype(jnp.int32))
    target = lax.broadcasted_iota(jnp.int32, (span_len, KEEP * BLK), 1)
    chosen = jnp.where(rank == target, 1.0, 0.0).astype(jnp.bfloat16)
    turn = turn_ref[place_ref[span]]
    keys = rotate(pool_ref[:, :width].astype(jnp.float32), turn[0:1], turn[1:2])
    kept = contract_first(chosen, keys.astype(jnp.bfloat16)).astype(jnp.bfloat16)
    vals = contract_first(pool_ref[:, width:], chosen).astype(jnp.bfloat16)
    for i in range(KEEP):
        for x in range(NX):
            keys_ref[x, i] = kept[i * BLK : (i + 1) * BLK]
        for z in range(NZ):
            vals_ref[z, i] = vals[:, i * BLK : (i + 1) * BLK]


def compact(slot_span, span_place, block_count, me, row_index, turn, pool):
    return pl.pallas_call(
        compact_kernel,
        in_specs=[SMEM, SMEM, SMEM, SMEM, VMEM, VMEM, VMEM],
        out_specs=(VMEM, VMEM),
        out_shape=(
            jax.ShapeDtypeStruct((NX, KEEP, BLK, BLK), pool.dtype),
            jax.ShapeDtypeStruct((NZ, KEEP, BLK, BLK), pool.dtype),
        ),
        name="compact",
    )(slot_span, span_place, block_count, me, row_index, turn, pool)


def load_weight(me_ref, weight_refs, buf, sems, steps):
    depth = buf.shape[1]
    cols = weight_refs[0].shape[1]
    copies = []
    for i, step in enumerate(steps):
        head = me_ref[1]
        head = ((head // 2 + step) % NY) * 2 + head % 2
        first = pl.multiple_of(head * depth, depth)
        for k, ref in enumerate(weight_refs):
            copy = pltpu.make_async_copy(
                ref.at[pl.ds(first, depth)], buf.at[i, :, pl.ds(k * cols, cols)], sems.at[i, k]
            )
            copy.start()
            copies.append(copy)
    return copies


NEAR = (0, -1, 1)
FAR = (2,)


def project_near_kernel(me_ref, *refs):
    n = len(NEAR)
    hid, weights, out_ref, buf, sems, hid_buf, hid_sems = refs[:n], refs[n : n + 2], *refs[n + 2 :]
    brought = [pltpu.make_async_copy(hid[i], hid_buf.at[i], hid_sems.at[i]) for i in range(n)]
    brought[0].start()
    copies = load_weight(me_ref, weights, buf, sems, NEAR)
    for c in brought[1:]:
        c.start()
    total = None
    for i in range(n):
        brought[i].wait()
        copies[2 * i].wait()
        copies[2 * i + 1].wait()
        part = jnp.dot(hid_buf[i], buf[i], preferred_element_type=jnp.float32)
        total = part if total is None else total + part
    out_ref[...] = total


def project_far_kernel(me_ref, top_ref, bottom_ref, mine_ref, other_ref, near_ref, out_ref, send_ref, buf, sems):
    copies = load_weight(me_ref, (mine_ref, other_ref), buf, sems, FAR)
    half = top_ref.shape[0]
    cols = out_ref.shape[1]
    for c in copies:
        c.wait()
    for b, ref in enumerate((top_ref, bottom_ref)):
        at = slice(b * half, (b + 1) * half)
        total = near_ref[at] + jnp.dot(ref[...], buf[0], preferred_element_type=jnp.float32)
        out_ref[at] = total[:, :cols]
        send_ref[at] = total[:, cols:]


def finish_kernel(mine_ref, got_ref, turn_ref, out_ref, chunk_ref):
    rows = out_ref.shape[0]
    width = out_ref.shape[1] // 2
    for b in range(rows // BLK):
        at = slice(b * BLK, (b + 1) * BLK)
        total = mine_ref[at] + got_ref[at]
        keys = rotate(total[:, :width], turn_ref[at, 0], turn_ref[at, 1]).astype(out_ref.dtype)
        out_ref[at, :width] = keys
        out_ref[at, width:] = total[:, width:].astype(out_ref.dtype)
        chunk_ref[b] = keys
        chunk_ref[2 + b] = total[:, width:].T.astype(out_ref.dtype)


def project(me, hidden, weight, other):
    near, far = hidden
    rows, depth = near[0].shape
    cols = weight.shape[1]
    params = pltpu.CompilerParams(vmem_limit_bytes=56 * 1024 * 1024)

    def scratch(n):
        return [
            pltpu.VMEM((n, depth, 2 * cols), weight.dtype),
            pltpu.SemaphoreType.DMA((n, 2)),
        ]

    partial = pl.pallas_call(
        project_near_kernel,
        in_specs=[SMEM] + [HBM] * (len(NEAR) + 2),
        out_specs=VMEM,
        out_shape=jax.ShapeDtypeStruct((rows, 2 * cols), jnp.float32),
        scratch_shapes=scratch(len(NEAR))
        + [
            pltpu.VMEM((len(NEAR), rows, depth), weight.dtype),
            pltpu.SemaphoreType.DMA((len(NEAR),)),
        ],
        compiler_params=params,
        name="project_near",
    )(me, *near, weight, other)
    half = jax.ShapeDtypeStruct((rows, cols), jnp.float32)
    return pl.pallas_call(
        project_far_kernel,
        in_specs=[SMEM] + [VMEM] * 2 + [HBM] * 2 + [VMEM],
        out_specs=(VMEM, VMEM),
        out_shape=(half, half),
        scratch_shapes=scratch(len(FAR)),
        compiler_params=params,
        name="project_far",
    )(me, *far, weight, other, partial)


def finish(mine, got, turn, kind):
    rows, cols = mine.shape
    return pl.pallas_call(
        finish_kernel,
        in_specs=[VMEM] * 3,
        out_specs=(VMEM, VMEM),
        out_shape=(
            jax.ShapeDtypeStruct((rows, cols), kind),
            jax.ShapeDtypeStruct((4, BLK, BLK), kind),
        ),
        name="finish",
    )(mine, got, turn)


class Scan:
    def __init__(self, q_scr, acc_scr, max_scr, sum_scr, blocks, per_block, factor):
        self.q, self.acc, self.max, self.sum = q_scr, acc_scr, max_scr, sum_scr
        self.blocks, self.per_block, self.factor = blocks, per_block, factor

    def tile(self, j, keys, vals, mask, first):
        scores = jnp.dot(keys, self.q[j], preferred_element_type=jnp.float32)
        if mask is not None:
            seen = mask(j // self.per_block, scores.shape)
            scores = jnp.where(seen, scores, -1e30)
        largest = jnp.max(scores, axis=0, keepdims=True)
        if not first:
            old = self.max[j]
            largest = jnp.maximum(old, largest)
        weights = jnp.exp2((scores - largest) * self.factor)
        if mask is not None:
            weights = jnp.where(seen, weights, 0.0)
        total = jnp.sum(weights, axis=0, keepdims=True)
        mixed = jnp.dot(vals, weights.astype(jnp.bfloat16), preferred_element_type=jnp.float32)
        if not first:
            shrink = jnp.exp2((old - largest) * self.factor)
            total = self.sum[j] * shrink + total
            mixed = self.acc[j] * shrink + mixed
        self.max[j] = largest
        self.sum[j] = total
        self.acc[j] = mixed

    def step(self, keys, vals, mask=None, first=False):
        keys = keys[0] if len(keys) == 1 else jnp.concatenate(keys, axis=0)
        vals = vals[0] if len(vals) == 1 else jnp.concatenate(vals, axis=1)

        def block(b, carry):
            for k in range(self.per_block):
                self.tile(b * self.per_block + k, keys, vals, mask, first)
            return carry

        lax.fori_loop(0, self.blocks, block, 0)

    def chunks(self, count, fetch):
        group = 4

        def many(g, carry):
            got = [fetch(g * group + i) for i in range(group)]
            self.step([k for k, _ in got], [v for _, v in got])
            return carry

        lax.fori_loop(0, count // group, many, 0)

        def one(i, carry):
            key, val = fetch(i)
            self.step([key], [val])
            return carry

        lax.fori_loop(count // group * group, count, one, 0)


def tables(slot_ref, place_ref, mine, by_place, owner_of):
    def fill(s, carry):
        owner_of[slot_ref[s]] = s

        @pl.when((s // 2) % 2 == mine)
        def _():
            by_place[place_ref[s]] = s

        return carry

    lax.fori_loop(0, slot_ref.shape[0], fill, 0)


def make_list(key_list, val_list, my_place, chunks_of):
    def add(p, count):
        key, val, number = chunks_of(p)

        def put(i, carry):
            key_list[count + i] = key + i
            val_list[count + i] = val + i
            return carry

        lax.fori_loop(0, number, put, 0)
        return count + number

    return lax.fori_loop(0, my_place, add, 0)


def attend_kernel(slot_ref, place_ref, count_ref, me_ref, q_ref, rows_ref, *refs):
    fresh_in, keys_in, vals_in, out_ref = refs[:NZ], refs[NZ : 2 * NZ], refs[2 * NZ : -13], refs[-13]
    by_place, owner_of, key_list, val_list, q_scr, acc_scr, max_scr, sum_scr = refs[-12:-4]
    fbuf, kbuf, vbuf, sems = refs[-4:]
    width = BLK
    rows = q_ref.shape[0]
    heads = q_ref.shape[1] // width
    me = me_ref[0]
    my_place = place_ref[me]
    copies = []

    def bring(source, target):
        copy = pltpu.make_async_copy(source, target, sems.at[len(copies)])
        copy.start()
        copies.append(copy)

    for d in range(NZ):
        bring(fresh_in[d], fbuf.at[d])
    for d in range(NZ):
        bring(keys_in[d], kbuf.at[pl.ds(d * NX, NX)])
    first = 0
    for ref in vals_in:
        bring(ref, vbuf.at[pl.ds(first, ref.shape[0])])
        first += ref.shape[0]
    tables(slot_ref, place_ref, (me // 2) % 2, by_place, owner_of)

    def fresh_at(span):
        e = jnp.where(span % NX == me % NX, 0, 1)
        at = ((span // NX - me // NX + NZ) % NZ) * 8 + e * 4
        return at, at + 2, count_ref[span]

    def cached_at(span):
        owner = owner_of[span]
        z = owner // NX
        d = (z - me // NX + NZ) % NZ
        e = (owner % NX - me % NX + NX) % NX
        return (d * NX + owner % NX) * KEEP, (e * NZ + z) * KEEP, 4 - count_ref[span]

    def fresh_chunk(c):
        return fbuf[c // 8, c % 8]

    def key_chunk(c):
        return kbuf[c // KEEP, c % KEEP]

    def val_chunk(c):
        return vbuf[c // KEEP, c % KEEP]

    count = make_list(key_list, val_list, my_place, lambda p: fresh_at(by_place[p]))
    for b in range(rows // BLK):
        for h in range(heads):
            piece = q_ref[b * BLK : (b + 1) * BLK, h * width : (h + 1) * width]
            q_scr[b * heads + h] = piece.T
    my_blocks = count_ref[me]
    scan = Scan(q_scr, acc_scr, max_scr, sum_scr, my_blocks, heads, width**-0.5 * LOG2E)

    def fresh_mask(block, shape):
        lane = lax.broadcasted_iota(jnp.int32, shape, 1)
        return lax.broadcasted_iota(jnp.int32, shape, 0) <= block * BLK + lane

    for c in copies[:NZ]:
        c.wait()
    scan.step([fbuf[0, 0], fbuf[0, 1]], [fbuf[0, 2], fbuf[0, 3]], fresh_mask, True)
    scan.chunks(count, lambda c: (fresh_chunk(key_list[c]), fresh_chunk(val_list[c])))
    count = make_list(key_list, val_list, my_place, lambda p: cached_at(by_place[p]))
    key_at, val_at, _ = cached_at(me)

    def cached_mask(block, shape):
        row = rows_ref[pl.ds(me, 1), :]
        row = row - lax.broadcasted_iota(jnp.int32, row.shape, 1)
        row = jnp.where(block == 0, row[:, :BLK], row[:, BLK:])
        return lax.broadcasted_iota(jnp.int32, shape, 0) < row

    for c in copies[NZ:]:
        c.wait()
    scan.step(
        [key_chunk(key_at + i) for i in range(KEEP)],
        [val_chunk(val_at + i) for i in range(KEEP)],
        cached_mask,
    )
    scan.chunks(count, lambda c: (key_chunk(key_list[c]), val_chunk(val_list[c])))
    for b in range(rows // BLK):

        @pl.when(b < my_blocks)
        def _():
            for h in range(heads):
                piece = acc_scr[b * heads + h] / sum_scr[b * heads + h]
                out_ref[b * BLK : (b + 1) * BLK, h * width : (h + 1) * width] = piece.T.astype(
                    out_ref.dtype
                )

        @pl.when(b >= my_blocks)
        def _():
            out_ref[b * BLK : (b + 1) * BLK, :] = jnp.zeros((BLK, heads * width), out_ref.dtype)


def attend(slot_span, span_place, block_count, me, queries, row_index, fresh, keys, vals):
    spans = slot_span.shape[0]
    tiles = queries.shape[0] * queries.shape[1] // BLK // LANES
    parts = len(fresh) + len(keys) + len(vals)
    return pl.pallas_call(
        attend_kernel,
        in_specs=[SMEM] * 4 + [VMEM] * 2 + [HBM] * parts,
        out_specs=VMEM,
        out_shape=jax.ShapeDtypeStruct(queries.shape, queries.dtype),
        scratch_shapes=[
            pltpu.SMEM((spans,), jnp.int32),
            pltpu.SMEM((spans,), jnp.int32),
            pltpu.SMEM((spans * KEEP,), jnp.int32),
            pltpu.SMEM((spans * KEEP,), jnp.int32),
            pltpu.VMEM((tiles, BLK, LANES), queries.dtype),
            pltpu.VMEM((tiles, BLK, LANES), jnp.float32),
            pltpu.VMEM((tiles, 1, LANES), jnp.float32),
            pltpu.VMEM((tiles, 1, LANES), jnp.float32),
            pltpu.VMEM((NZ, 8, BLK, BLK), queries.dtype),
            pltpu.VMEM((spans, KEEP, BLK, BLK), queries.dtype),
            pltpu.VMEM((spans, KEEP, BLK, BLK), queries.dtype),
            pltpu.SemaphoreType.DMA((parts,)),
        ],
        compiler_params=pltpu.CompilerParams(vmem_limit_bytes=56 * 1024 * 1024),
        name="attend",
    )(slot_span, span_place, block_count, me, queries, row_index, *fresh, *keys, *vals)


def shift_ctx(values, dz, dx):
    pairs = [
        (((z + dz) % NZ) * NX + (x + dx) % NX, z * NX + x) for z in range(NZ) for x in range(NX)
    ]
    return lax.ppermute(values, "ctx", pairs)


def swap_ctx(values):
    pairs = [(z * NX + (x ^ 1), z * NX + x) for z in range(NZ) for x in range(NX)]
    return lax.ppermute(values, "ctx", pairs)


def shift_head(values, dy):
    pairs = [(((y + dy) % NY) * 2 + c, y * 2 + c) for y in range(NY) for c in range(2)]
    return lax.ppermute(values, "head", pairs)


def swap_core(values):
    pairs = [(y * 2 + 1 - c, y * 2 + c) for y in range(NY) for c in range(2)]
    return lax.ppermute(values, "head", pairs)


def around(up, down):
    return shift_ctx(up, 1, 0), shift_ctx(down, -1, 0)


ROWS_OF_CHIPS = [[z * NX + x for x in range(NX)] for z in range(NZ)]
COLUMNS_OF_CHIPS = [[z * NX + x for z in range(NZ)] for x in range(NX)]


def together(*values):
    return lax.optimization_barrier(values)


def shards(hidden_rows, kv_weight, queries, kv_pool, slot_span, span_place, row_index, block_count):
    width = kv_weight.shape[1] // 2
    span_len = kv_pool.shape[0]
    spans = span_place.shape[0]
    position = lax.axis_index("ctx")
    me = jnp.stack([position, lax.axis_index("head")]).astype(jnp.int32)
    my_pos = span_place[position] * span_len + lax.dynamic_index_in_dim(
        row_index, position, 0, keepdims=False
    )
    turn = jnp.asarray(place_table(spans // 2, span_len, width))
    other = swap_core(kv_weight)
    low = shift_head(hidden_rows, -1)
    high = shift_head(hidden_rows, 1)
    keys, vals = compact(slot_span, span_place, block_count, me, row_index, turn, kv_pool)
    row_keys = lax.all_to_all(keys, "ctx", 0, 0, axis_index_groups=ROWS_OF_CHIPS)
    column = lax.all_to_all(vals, "ctx", 0, 0, axis_index_groups=COLUMNS_OF_CHIPS)

    half = hidden_rows.shape[0] // 2
    far = (shift_head(low[:half], -1), shift_head(high[half:], 1))
    mine, send = project(me, ((hidden_rows, low, high), far), kv_weight, other)
    send, row_keys = together(send, row_keys)
    k1, k7 = around(row_keys, row_keys)
    fresh, chunks = finish(mine, swap_core(send), rope_table(my_pos, width), kv_weight.dtype)
    pair = swap_ctx(chunks)
    column, pair = together(column, pair)
    right = shift_ctx(column, 0, 1)
    left = shift_ctx(column, 0, -1)
    both = jnp.concatenate([chunks, pair], axis=0)
    f1, f7 = around(both, both)
    k2, k6 = around(k1, k7)
    right, left, f1, f7, k2, k6 = together(right, left, f1, f7, k2, k6)
    across = (shift_ctx(right[: NZ // 2], 0, 1), shift_ctx(left[NZ // 2 :], 0, -1))
    f2, f6 = around(f1, f7)
    f3, f5 = around(f2, f6)
    f4 = shift_ctx(f3, 1, 0)
    k3, k5 = around(k2, k6)
    k4 = shift_ctx(k5, -1, 0)
    all_fresh = (both, f1, f2, f3, f4, f5, f6, f7)
    all_keys = (row_keys, k1, k2, k3, k4, k5, k6, k7)
    all_vals = (column, right, *across, left)
    attended = attend(
        slot_span,
        span_place,
        block_count,
        me,
        queries,
        row_index,
        all_fresh,
        all_keys,
        all_vals,
    )
    return fresh, attended


def solution(mesh):
    in_specs = (
        P("ctx", "head"),
        P(None, "head"),
        P("ctx", "head"),
        P("ctx", "head"),
        P(),
        P(),
        P(),
        P(),
    )
    out_specs = (P("ctx", "head"), P("ctx", "head"))
    return jax.shard_map(shards, mesh=mesh, in_specs=in_specs, out_specs=out_specs, check_vma=False)
```

```python
import math

import jax
import jax.numpy as jnp
import numpy as np
from jax import lax
from jax.experimental import pallas as pl
from jax.experimental.pallas import tpu as pltpu
from jax.sharding import PartitionSpec as P

BLK = 128
LANES = 128
NX = 4
NZ = 8
NY = 4
KEEP = 3
LOG2E = 1.4426950408889634

SMEM = pl.BlockSpec(memory_space=pltpu.SMEM)
VMEM = pl.BlockSpec(memory_space=pltpu.VMEM)
HBM = pl.BlockSpec(memory_space=pl.ANY)


def rope_freqs(size):
    half = size // 2
    base = 500000.0 ** (-2.0 * jnp.arange(half, dtype=jnp.float32) / size)
    wavelen = 2.0 * math.pi / base
    smooth = (8192.0 / wavelen - 1.0) / 3.0
    blended = (1.0 - smooth) * base / 8.0 + smooth * base
    return jnp.where(wavelen < 2048.0, base, jnp.where(wavelen > 8192.0, base / 8.0, blended))


def rope_table(positions, size):
    angles = positions.astype(jnp.float32)[:, None] * rope_freqs(size)[None, :]
    cosine, sine = jnp.cos(angles), jnp.sin(angles)
    return jnp.stack(
        [jnp.concatenate([cosine, cosine], 1), jnp.concatenate([-sine, sine], 1)], axis=1
    )


def place_table(places, span_len, size):
    half = size // 2
    base = 500000.0 ** (-2.0 * np.arange(half) / size)
    wavelen = 2.0 * math.pi / base
    smooth = (8192.0 / wavelen - 1.0) / 3.0
    blended = (1.0 - smooth) * base / 8.0 + smooth * base
    freqs = np.where(wavelen < 2048.0, base, np.where(wavelen > 8192.0, base / 8.0, blended))
    positions = np.arange(places, dtype=np.float32) * span_len
    angles = (positions[:, None] * freqs.astype(np.float32)[None, :]).astype(np.float64)
    cosine, sine = np.cos(angles), np.sin(angles)
    table = np.stack([np.concatenate([cosine, cosine], 1), np.concatenate([-sine, sine], 1)], 1)
    return table.astype(np.float32)


def rotate(keys, cosine, sine):
    return keys * cosine + pltpu.roll(keys, keys.shape[-1] // 2, 1) * sine


def contract_first(a, b):
    return lax.dot_general(a, b, (((0,), (0,)), ((), ())), preferred_element_type=jnp.float32)


def compact_kernel(slot_ref, place_ref, count_ref, me_ref, rows_ref, turn_ref, pool_ref, keys_ref, vals_ref):
    span_len = pool_ref.shape[0]
    width = pool_ref.shape[1] // 2
    rows = rows_ref.shape[1]
    span = slot_ref[me_ref[0]]
    live = count_ref[span] * BLK
    picks = rows_ref[pl.ds(span, 1), :]
    lane = lax.broadcasted_iota(jnp.int32, (1, rows), 1)
    picks = jnp.where(lane < live, picks, 4 * span_len)
    here = lax.broadcasted_iota(jnp.int32, (span_len, rows), 0)
    before = jnp.sum((picks < here).astype(jnp.float32), axis=1, keepdims=True)
    gone = jnp.sum((picks == here).astype(jnp.float32), axis=1, keepdims=True)
    row = lax.broadcasted_iota(jnp.int32, (span_len, 1), 0)
    rank = jnp.where(gone > 0.5, -1, row - before.astype(jnp.int32))
    target = lax.broadcasted_iota(jnp.int32, (span_len, KEEP * BLK), 1)
    chosen = jnp.where(rank == target, 1.0, 0.0).astype(jnp.bfloat16)
    turn = turn_ref[place_ref[span]]
    keys = rotate(pool_ref[:, :width].astype(jnp.float32), turn[0:1], turn[1:2])
    kept = contract_first(chosen, keys.astype(jnp.bfloat16)).astype(jnp.bfloat16)
    vals = contract_first(pool_ref[:, width:], chosen).astype(jnp.bfloat16)
    for i in range(KEEP):
        for x in range(NX):
            keys_ref[x, i] = kept[i * BLK : (i + 1) * BLK]
        for z in range(NZ):
            vals_ref[z, i] = vals[:, i * BLK : (i + 1) * BLK]


def compact(slot_span, span_place, block_count, me, row_index, turn, pool):
    return pl.pallas_call(
        compact_kernel,
        in_specs=[SMEM, SMEM, SMEM, SMEM, VMEM, VMEM, VMEM],
        out_specs=(VMEM, VMEM),
        out_shape=(
            jax.ShapeDtypeStruct((NX, KEEP, BLK, BLK), pool.dtype),
            jax.ShapeDtypeStruct((NZ, KEEP, BLK, BLK), pool.dtype),
        ),
        cost_estimate=pl.CostEstimate(flops=10**10, bytes_accessed=2**20, transcendentals=0),
        name="compact",
    )(slot_span, span_place, block_count, me, row_index, turn, pool)


def load_weight(me_ref, weight_refs, buf, sems, steps):
    depth = buf.shape[1]
    cols = weight_refs[0].shape[1]
    copies = []
    for i, step in enumerate(steps):
        head = me_ref[1]
        head = ((head // 2 + step) % NY) * 2 + head % 2
        first = pl.multiple_of(head * depth, depth)
        for k, ref in enumerate(weight_refs):
            copy = pltpu.make_async_copy(
                ref.at[pl.ds(first, depth)], buf.at[i, :, pl.ds(k * cols, cols)], sems.at[i, k]
            )
            copy.start()
            copies.append(copy)
    return copies


NEAR = (0, -1, 1)
FAR = (2,)


def project_near_kernel(me_ref, *refs):
    n = len(NEAR)
    hid, weights, out_ref, buf, sems, hid_buf, hid_sems = refs[:n], refs[n : n + 2], *refs[n + 2 :]
    brought = [pltpu.make_async_copy(hid[i], hid_buf.at[i], hid_sems.at[i]) for i in range(n)]
    brought[0].start()
    copies = load_weight(me_ref, weights, buf, sems, NEAR)
    for c in brought[1:]:
        c.start()
    total = None
    for i in range(n):
        brought[i].wait()
        copies[2 * i].wait()
        copies[2 * i + 1].wait()
        part = jnp.dot(hid_buf[i], buf[i], preferred_element_type=jnp.float32)
        total = part if total is None else total + part
    out_ref[...] = total


def project_far_kernel(me_ref, top_ref, bottom_ref, mine_ref, other_ref, near_ref, out_ref, send_ref, buf, sems):
    copies = load_weight(me_ref, (mine_ref, other_ref), buf, sems, FAR)
    half = top_ref.shape[0]
    cols = out_ref.shape[1]
    for c in copies:
        c.wait()
    for b, ref in enumerate((top_ref, bottom_ref)):
        at = slice(b * half, (b + 1) * half)
        total = near_ref[at] + jnp.dot(ref[...], buf[0], preferred_element_type=jnp.float32)
        out_ref[at] = total[:, :cols]
        send_ref[at] = total[:, cols:]


def finish_kernel(mine_ref, got_ref, turn_ref, out_ref, chunk_ref):
    rows = out_ref.shape[0]
    width = out_ref.shape[1] // 2
    for b in range(rows // BLK):
        at = slice(b * BLK, (b + 1) * BLK)
        total = mine_ref[at] + got_ref[at]
        keys = rotate(total[:, :width], turn_ref[at, 0], turn_ref[at, 1]).astype(out_ref.dtype)
        out_ref[at, :width] = keys
        out_ref[at, width:] = total[:, width:].astype(out_ref.dtype)
        chunk_ref[b] = keys
        chunk_ref[2 + b] = total[:, width:].T.astype(out_ref.dtype)


def project(me, hidden, weight, other):
    near, far = hidden
    rows, depth = near[0].shape
    cols = weight.shape[1]
    params = pltpu.CompilerParams(vmem_limit_bytes=56 * 1024 * 1024)

    def scratch(n):
        return [
            pltpu.VMEM((n, depth, 2 * cols), weight.dtype),
            pltpu.SemaphoreType.DMA((n, 2)),
        ]

    partial = pl.pallas_call(
        project_near_kernel,
        in_specs=[SMEM] + [HBM] * (len(NEAR) + 2),
        out_specs=VMEM,
        out_shape=jax.ShapeDtypeStruct((rows, 2 * cols), jnp.float32),
        scratch_shapes=scratch(len(NEAR))
        + [
            pltpu.VMEM((len(NEAR), rows, depth), weight.dtype),
            pltpu.SemaphoreType.DMA((len(NEAR),)),
        ],
        compiler_params=params,
        name="project_near",
    )(me, *near, weight, other)
    half = jax.ShapeDtypeStruct((rows, cols), jnp.float32)
    return pl.pallas_call(
        project_far_kernel,
        in_specs=[SMEM] + [VMEM] * 2 + [HBM] * 2 + [VMEM],
        out_specs=(VMEM, VMEM),
        out_shape=(half, half),
        scratch_shapes=scratch(len(FAR)),
        compiler_params=params,
        name="project_far",
    )(me, *far, weight, other, partial)


def finish(mine, got, turn, kind):
    rows, cols = mine.shape
    return pl.pallas_call(
        finish_kernel,
        in_specs=[VMEM] * 3,
        out_specs=(VMEM, VMEM),
        out_shape=(
            jax.ShapeDtypeStruct((rows, cols), kind),
            jax.ShapeDtypeStruct((4, BLK, BLK), kind),
        ),
        name="finish",
    )(mine, got, turn)


class Scan:
    def __init__(self, q_scr, acc_scr, max_scr, sum_scr, blocks, per_block, factor):
        self.q, self.acc, self.max, self.sum = q_scr, acc_scr, max_scr, sum_scr
        self.blocks, self.per_block, self.factor = blocks, per_block, factor

    def tile(self, j, keys, vals, mask, first):
        scores = jnp.dot(keys, self.q[j], preferred_element_type=jnp.float32)
        if mask is not None:
            seen = mask(j // self.per_block, scores.shape)
            scores = jnp.where(seen, scores, -1e30)
        largest = jnp.max(scores, axis=0, keepdims=True)
        if not first:
            old = self.max[j]
            largest = jnp.maximum(old, largest)
        weights = jnp.exp2((scores - largest) * self.factor)
        if mask is not None:
            weights = jnp.where(seen, weights, 0.0)
        total = jnp.sum(weights, axis=0, keepdims=True)
        mixed = jnp.dot(vals, weights.astype(jnp.bfloat16), preferred_element_type=jnp.float32)
        if not first:
            shrink = jnp.exp2((old - largest) * self.factor)
            total = self.sum[j] * shrink + total
            mixed = self.acc[j] * shrink + mixed
        self.max[j] = largest
        self.sum[j] = total
        self.acc[j] = mixed

    def step(self, keys, vals, mask=None, first=False):
        keys = keys[0] if len(keys) == 1 else jnp.concatenate(keys, axis=0)
        vals = vals[0] if len(vals) == 1 else jnp.concatenate(vals, axis=1)

        def block(b, carry):
            for k in range(self.per_block):
                self.tile(b * self.per_block + k, keys, vals, mask, first)
            return carry

        lax.fori_loop(0, self.blocks, block, 0)

    def chunks(self, count, fetch):
        group = 4

        def many(g, carry):
            got = [fetch(g * group + i) for i in range(group)]
            self.step([k for k, _ in got], [v for _, v in got])
            return carry

        lax.fori_loop(0, count // group, many, 0)

        def one(i, carry):
            key, val = fetch(i)
            self.step([key], [val])
            return carry

        lax.fori_loop(count // group * group, count, one, 0)


def tables(slot_ref, place_ref, mine, by_place, owner_of):
    def fill(s, carry):
        owner_of[slot_ref[s]] = s

        @pl.when((s // 2) % 2 == mine)
        def _():
            by_place[place_ref[s]] = s

        return carry

    lax.fori_loop(0, slot_ref.shape[0], fill, 0)


def make_list(key_list, val_list, my_place, chunks_of):
    def add(p, count):
        key, val, number = chunks_of(p)

        def put(i, carry):
            key_list[count + i] = key + i
            val_list[count + i] = val + i
            return carry

        lax.fori_loop(0, number, put, 0)
        return count + number

    return lax.fori_loop(0, my_place, add, 0)


def attend_kernel(slot_ref, place_ref, count_ref, me_ref, q_ref, rows_ref, *refs):
    fresh_in, keys_in, vals_in, out_ref = refs[:NZ], refs[NZ : 2 * NZ], refs[2 * NZ : -13], refs[-13]
    by_place, owner_of, key_list, val_list, q_scr, acc_scr, max_scr, sum_scr = refs[-12:-4]
    fbuf, kbuf, vbuf, sems = refs[-4:]
    width = BLK
    rows = q_ref.shape[0]
    heads = q_ref.shape[1] // width
    me = me_ref[0]
    my_place = place_ref[me]
    copies = []

    def bring(source, target):
        copy = pltpu.make_async_copy(source, target, sems.at[len(copies)])
        copy.start()
        copies.append(copy)

    for d in range(NZ):
        bring(fresh_in[d], fbuf.at[d])
    for d in range(NZ):
        bring(keys_in[d], kbuf.at[pl.ds(d * NX, NX)])
    first = 0
    for ref in vals_in:
        bring(ref, vbuf.at[pl.ds(first, ref.shape[0])])
        first += ref.shape[0]
    tables(slot_ref, place_ref, (me // 2) % 2, by_place, owner_of)

    def fresh_at(span):
        e = jnp.where(span % NX == me % NX, 0, 1)
        at = ((span // NX - me // NX + NZ) % NZ) * 8 + e * 4
        return at, at + 2, count_ref[span]

    def cached_at(span):
        owner = owner_of[span]
        z = owner // NX
        d = (z - me // NX + NZ) % NZ
        e = (owner % NX - me % NX + NX) % NX
        return (d * NX + owner % NX) * KEEP, (e * NZ + z) * KEEP, 4 - count_ref[span]

    def fresh_chunk(c):
        return fbuf[c // 8, c % 8]

    def key_chunk(c):
        return kbuf[c // KEEP, c % KEEP]

    def val_chunk(c):
        return vbuf[c // KEEP, c % KEEP]

    count = make_list(key_list, val_list, my_place, lambda p: fresh_at(by_place[p]))
    for b in range(rows // BLK):
        for h in range(heads):
            piece = q_ref[b * BLK : (b + 1) * BLK, h * width : (h + 1) * width]
            q_scr[b * heads + h] = piece.T
    my_blocks = count_ref[me]
    scan = Scan(q_scr, acc_scr, max_scr, sum_scr, my_blocks, heads, width**-0.5 * LOG2E)

    def fresh_mask(block, shape):
        lane = lax.broadcasted_iota(jnp.int32, shape, 1)
        return lax.broadcasted_iota(jnp.int32, shape, 0) <= block * BLK + lane

    for c in copies[:NZ]:
        c.wait()
    scan.step([fbuf[0, 0], fbuf[0, 1]], [fbuf[0, 2], fbuf[0, 3]], fresh_mask, True)
    scan.chunks(count, lambda c: (fresh_chunk(key_list[c]), fresh_chunk(val_list[c])))
    count = make_list(key_list, val_list, my_place, lambda p: cached_at(by_place[p]))
    key_at, val_at, _ = cached_at(me)

    def cached_mask(block, shape):
        row = rows_ref[pl.ds(me, 1), :]
        row = row - lax.broadcasted_iota(jnp.int32, row.shape, 1)
        row = jnp.where(block == 0, row[:, :BLK], row[:, BLK:])
        return lax.broadcasted_iota(jnp.int32, shape, 0) < row

    for c in copies[NZ:]:
        c.wait()
    scan.step(
        [key_chunk(key_at + i) for i in range(KEEP)],
        [val_chunk(val_at + i) for i in range(KEEP)],
        cached_mask,
    )
    scan.chunks(count, lambda c: (key_chunk(key_list[c]), val_chunk(val_list[c])))
    for b in range(rows // BLK):

        @pl.when(b < my_blocks)
        def _():
            for h in range(heads):
                piece = acc_scr[b * heads + h] / sum_scr[b * heads + h]
                out_ref[b * BLK : (b + 1) * BLK, h * width : (h + 1) * width] = piece.T.astype(
                    out_ref.dtype
                )

        @pl.when(b >= my_blocks)
        def _():
            out_ref[b * BLK : (b + 1) * BLK, :] = jnp.zeros((BLK, heads * width), out_ref.dtype)


def attend(slot_span, span_place, block_count, me, queries, row_index, fresh, keys, vals):
    spans = slot_span.shape[0]
    tiles = queries.shape[0] * queries.shape[1] // BLK // LANES
    parts = len(fresh) + len(keys) + len(vals)
    return pl.pallas_call(
        attend_kernel,
        in_specs=[SMEM] * 4 + [VMEM] * 2 + [HBM] * parts,
        out_specs=VMEM,
        out_shape=jax.ShapeDtypeStruct(queries.shape, queries.dtype),
        scratch_shapes=[
            pltpu.SMEM((spans,), jnp.int32),
            pltpu.SMEM((spans,), jnp.int32),
            pltpu.SMEM((spans * KEEP,), jnp.int32),
            pltpu.SMEM((spans * KEEP,), jnp.int32),
            pltpu.VMEM((tiles, BLK, LANES), queries.dtype),
            pltpu.VMEM((tiles, BLK, LANES), jnp.float32),
            pltpu.VMEM((tiles, 1, LANES), jnp.float32),
            pltpu.VMEM((tiles, 1, LANES), jnp.float32),
            pltpu.VMEM((NZ, 8, BLK, BLK), queries.dtype),
            pltpu.VMEM((spans, KEEP, BLK, BLK), queries.dtype),
            pltpu.VMEM((spans, KEEP, BLK, BLK), queries.dtype),
            pltpu.SemaphoreType.DMA((parts,)),
        ],
        compiler_params=pltpu.CompilerParams(vmem_limit_bytes=56 * 1024 * 1024),
        name="attend",
    )(slot_span, span_place, block_count, me, queries, row_index, *fresh, *keys, *vals)


def shift_ctx(values, dz, dx):
    pairs = [
        (((z + dz) % NZ) * NX + (x + dx) % NX, z * NX + x) for z in range(NZ) for x in range(NX)
    ]
    return lax.ppermute(values, "ctx", pairs)


def swap_ctx(values):
    pairs = [(z * NX + (x ^ 1), z * NX + x) for z in range(NZ) for x in range(NX)]
    return lax.ppermute(values, "ctx", pairs)


def shift_head(values, dy):
    pairs = [(((y + dy) % NY) * 2 + c, y * 2 + c) for y in range(NY) for c in range(2)]
    return lax.ppermute(values, "head", pairs)


def swap_core(values):
    pairs = [(y * 2 + 1 - c, y * 2 + c) for y in range(NY) for c in range(2)]
    return lax.ppermute(values, "head", pairs)


def around(up, down):
    return shift_ctx(up, 1, 0), shift_ctx(down, -1, 0)


ROWS_OF_CHIPS = [[z * NX + x for x in range(NX)] for z in range(NZ)]
COLUMNS_OF_CHIPS = [[z * NX + x for z in range(NZ)] for x in range(NX)]


def together(*values):
    return lax.optimization_barrier(values)


def shards(hidden_rows, kv_weight, queries, kv_pool, slot_span, span_place, row_index, block_count):
    width = kv_weight.shape[1] // 2
    span_len = kv_pool.shape[0]
    spans = span_place.shape[0]
    position = lax.axis_index("ctx")
    me = jnp.stack([position, lax.axis_index("head")]).astype(jnp.int32)
    my_pos = span_place[position] * span_len + lax.dynamic_index_in_dim(
        row_index, position, 0, keepdims=False
    )
    turn = jnp.asarray(place_table(spans // 2, span_len, width))
    other = swap_core(kv_weight)
    low = shift_head(hidden_rows, -1)
    high = shift_head(hidden_rows, 1)
    keys, vals = compact(slot_span, span_place, block_count, me, row_index, turn, kv_pool)
    row_keys = lax.all_to_all(keys, "ctx", 0, 0, axis_index_groups=ROWS_OF_CHIPS)
    column = lax.all_to_all(vals, "ctx", 0, 0, axis_index_groups=COLUMNS_OF_CHIPS)

    half = hidden_rows.shape[0] // 2
    far = (shift_head(low[:half], -1), shift_head(high[half:], 1))
    mine, send = project(me, ((hidden_rows, low, high), far), kv_weight, other)
    send, row_keys = together(send, row_keys)
    k1, k7 = around(row_keys, row_keys)
    fresh, chunks = finish(mine, swap_core(send), rope_table(my_pos, width), kv_weight.dtype)
    pair = swap_ctx(chunks)
    column, pair = together(column, pair)
    right = shift_ctx(column, 0, 1)
    left = shift_ctx(column, 0, -1)
    both = jnp.concatenate([chunks, pair], axis=0)
    f1, f7 = around(both, both)
    k2, k6 = around(k1, k7)
    right, left, f1, f7, k2, k6 = together(right, left, f1, f7, k2, k6)
    across = (shift_ctx(right[: NZ // 2], 0, 1), shift_ctx(left[NZ // 2 :], 0, -1))
    f2, f6 = around(f1, f7)
    f3, f5 = around(f2, f6)
    f4 = shift_ctx(f3, 1, 0)
    k3, k5 = around(k2, k6)
    k4 = shift_ctx(k5, -1, 0)
    all_fresh = (both, f1, f2, f3, f4, f5, f6, f7)
    all_keys = (row_keys, k1, k2, k3, k4, k5, k6, k7)
    all_vals = (column, right, *across, left)
    attended = attend(
        slot_span,
        span_place,
        block_count,
        me,
        queries,
        row_index,
        all_fresh,
        all_keys,
        all_vals,
    )
    return fresh, attended


def solution(mesh):
    in_specs = (
        P("ctx", "head"),
        P(None, "head"),
        P("ctx", "head"),
        P("ctx", "head"),
        P(),
        P(),
        P(),
        P(),
    )
    out_specs = (P("ctx", "head"), P("ctx", "head"))
    return jax.shard_map(shards, mesh=mesh, in_specs=in_specs, out_specs=out_specs, check_vma=False)
```
